128 devices in a mesh: horiz: 32 (over z, x, core), depth: 4 (over y).
Axes of the slice: x: 4, y: 4, z: 4, core: 2. Of those that a mesh axis runs over, the one named last changes fastest.
Arguments:
- adjoint_seed: bfloat16 [16, 48, 32768], P(None, 'depth', 'horiz'), may hold values from -6 to 6
- transport: bfloat16 [48, 256, 5, 128, 128], P('depth', 'horiz'), may hold values from -0.25 to 0.25
- neighbours: int32 [256, 5], P('horiz'), may hold values from 0 to 255, as said below
- inv_mix: float32 [48, 48, 32768], P(None, None, ('horiz', 'depth')), may hold values from -0.875 to 0.875
- rates: float32 [48, 32768], P('depth', 'horiz'), may hold values from 0.2 to 2
- coupling: float32 [16, 16], replicated, may hold values from -1.5 to 1.5
- sensitivity: bfloat16 [16, 48, 32768], P(None, 'depth', 'horiz')
- depth_count: int32 [32768], P('horiz'), may hold values from 0 to 48, as said below
Outputs:
- first: bfloat16 [16, 48, 32768], P(None, 'depth', 'horiz')
- second: bfloat16 [16, 48, 32768], P(None, 'depth', 'horiz')
- gradient: float32 [16], replicated
The draws below stay inside these ranges and needn't reach their ends.
Inputs may be any that keep to these rules, and one draw needn't show every extreme that they name: neighbours[b, 0] = b; every entry lies within 8 blocks of its row's block b, counted cyclically over 256 blocks. `depth_count`: 0 marks a land column.
All inputs are finite; a program needn't handle non-finite values.
Results may differ from the reference program's by a relative error of at most 0.011.
Values may be sent and summed in bfloat16 or wider, within the bound.
No kernel may reach another device: no remote copies, remote signals or barrier semaphores. Data moves between devices by JAX's collectives and lax.ppermute only.
A program may use at most 128 MiB of HBM per device.

```python
import math
import jax
import jax.numpy as jnp
from jax import lax

TR = 16
L = 48
COLBLK = 128
K = 5
BLK_DEV = 8
NBLK = 256
COLS = 32768


def draw_neighbours(key, part):
    key = jax.random.fold_in(key, 11)
    reach = BLK_DEV
    offsets = jax.random.randint(key, (NBLK, K), -reach, reach + 1)
    row_ids = jnp.arange(NBLK, dtype=jnp.int32)
    offsets = offsets.at[:, 0].set(0)
    marked = row_ids % BLK_DEV == 0
    offsets = offsets.at[:, 1].set(jnp.where(marked, reach, offsets[:, 1]))
    offsets = offsets.at[:, 2].set(jnp.where(marked, -reach, offsets[:, 2]))
    return ((row_ids[:, None] + offsets) % NBLK).astype(jnp.int32)


def draw_depth_count(key, part):
    key = jax.random.fold_in(key, 12)
    key_land, key_levels = jax.random.split(key)
    land = jax.random.randint(key_land, (COLS,), 0, 10) < 3
    levels = jax.random.randint(key_levels, (COLS,), 1, L + 1)
    levels = levels.at[1].set(L)
    counts = jnp.where(land, 0, levels)
    counts = counts.at[0].set(0)
    return counts.astype(jnp.int32)


def draw_sensitivity(key, part):
    key = jax.random.fold_in(key, 13)
    key_main = jax.random.fold_in(key, 0)
    position = jnp.arange(COLS, dtype=jnp.float32) / COLS
    growth = (1.0 + 2.0 * position)[None, None, :]
    values = jax.random.normal(key_main, (TR, L, COLS), jnp.float32) * growth
    return values.astype(jnp.bfloat16)


def block_levels(rng, extent, pieces, least, high):
    def one(dim, shards_of):
        steps = jax.random.uniform(jax.random.fold_in(jax.random.fold_in(rng, 6), dim), (shards_of,), jnp.float32, least / len(pieces), high / len(pieces))
        return jnp.repeat(jnp.exp(steps), extent[dim] // shards_of).reshape((-1,) + (1,) * (len(extent) - dim - 1))

    factor_of = one(*pieces[0])
    for cut in pieces[1:]:
        factor_of = factor_of * one(*cut)
    return factor_of


def centred(key, dims, width, most, shards=(), kind=jnp.bfloat16):
    drawn = jax.random.normal(key, dims, jnp.float32) * width
    if len(shards) > 0:
        drawn = block_levels(key, dims, shards, -0.22, 0.18) * drawn
    return jnp.clip(drawn, min=-most, max=most).astype(kind)


def setup_inputs(seed: int = 0) -> dict:
    arg_keys = jax.random.split(jax.random.key(seed), 9)
    return {
        "adjoint_seed": centred(arg_keys[0], (TR, L, COLS), 1.0, 6.0, ((1, 4), (2, 32))),
        "transport": centred(arg_keys[1], (L, NBLK, K, COLBLK, COLBLK), (K * COLBLK) ** -0.5, 0.25, ((0, 4), (1, 32))),
        "neighbours": draw_neighbours(jax.random.fold_in(arg_keys[8], 71), 0),
        "inv_mix": centred(arg_keys[3], (L, L, COLS), L ** -0.5, 0.875, ((2, 128),), jnp.float32),
        "rates": jnp.clip(jnp.exp(math.log(2.0) - 2.3025851 * jax.random.uniform(arg_keys[4], (L, COLS), jnp.float32) ** block_levels(arg_keys[4], (L, COLS), ((0, 4), (1, 32)), -0.2, 0.2)), 0.2, 2.0),
        "coupling": centred(arg_keys[5], (TR, TR), TR ** -0.5, 1.5, (), jnp.float32),
        "sensitivity": draw_sensitivity(jax.random.fold_in(arg_keys[8], 71), 0),
        "depth_count": draw_depth_count(jax.random.fold_in(arg_keys[8], 71), 0),
    }


def reference(adjoint_seed, transport, neighbours, inv_mix, rates, coupling, sensitivity, depth_count):
    level_ids = jnp.arange(L, dtype=jnp.int32)[:, None]
    wet = (level_ids < depth_count[None, :]).astype(jnp.float32)
    state = adjoint_seed
    results = []
    grad_total = jnp.zeros((TR,), jnp.float32)
    sens = sensitivity.astype(jnp.float32)
    for step in range(2):
        mixed = jnp.einsum('pqc,tpc->tqc', inv_mix, state.astype(jnp.float32), precision=lax.Precision.HIGHEST).astype(jnp.bfloat16)
        mixed_f = mixed.astype(jnp.float32)
        by_level = jnp.transpose(mixed.reshape(TR, L, NBLK, COLBLK), (1, 0, 2, 3))

        def level_fn(pair):
            weights, level_vec = pair
            picked = level_vec[:, neighbours]
            return jnp.einsum('bkij,tbkj->tbi', weights.astype(jnp.float32), picked.astype(jnp.float32), precision=lax.Precision.HIGHEST)
        moved = lax.map(level_fn, (transport, by_level))
        moved = jnp.transpose(moved, (1, 0, 2, 3)).reshape(TR, L, COLS)
        source_term = rates[None, :, :] * jnp.einsum('ut,ulc->tlc', coupling, mixed_f, precision=lax.Precision.HIGHEST)
        new_state = (wet[None] * (moved + source_term - state.astype(jnp.float32))).astype(jnp.bfloat16)
        grad_total = grad_total + lax.optimization_barrier(jnp.sum(wet[None] * mixed_f * sens, axis=(1, 2)))
        results.append(new_state)
        state = new_state
    gradient = grad_total / math.sqrt(L * COLS)
    return (results[0], results[1], gradient)
```

```python
import functools
import math

import jax
import jax.numpy as jnp
from jax import lax
from jax.experimental import pallas as pl
from jax.experimental.pallas import tpu as pltpu
from jax.sharding import PartitionSpec as P

VMEM = pl.BlockSpec(memory_space=pltpu.VMEM)
SMEM = pl.BlockSpec(memory_space=pltpu.SMEM)
HBM = pl.BlockSpec(memory_space=pltpu.HBM)
MIB = 1024 * 1024
GROUP = 4


def split_kernel(place, state, sens, *refs):
    parts, sem = refs[:-1], refs[-1]
    depth, levels, width = len(parts), state.shape[0], parts[0].shape[2]
    copies = []
    for s in range(depth):
        start = pl.multiple_of(lax.rem(place[0] + s, depth) * width, width)
        for i, whole in enumerate((state, sens)):
            copies.append(
                pltpu.make_async_copy(
                    whole.at[:, :, pl.ds(start, width)],
                    parts[s].at[pl.ds(i * levels, levels)],
                    sem.at[2 * s + i],
                )
            )
    for copy in copies:
        copy.start()
    for copy in copies:
        copy.wait()


def list_entries(place, neighbours, entries, total_blocks):
    blocks, slots = neighbours.shape
    half = entries.shape[1] // 2
    odd = place[1]
    counts = (jnp.int32(0), jnp.int32(0))
    for b in range(blocks):
        row = place[2] * blocks + b
        for k in range(slots):
            ahead = lax.rem(neighbours[b, k] - row + blocks + total_blocks, total_blocks)
            source = b + jnp.clip(ahead, 0, 2 * blocks)
            beside = lax.div(source, blocks)
            far = (beside == 2 * odd).astype(jnp.int32)
            at = jnp.where(far == 1, half + counts[1], counts[0])
            entries[0, at] = b * slots + k
            entries[1, at] = b
            entries[2, at] = jnp.where(far == 1, source - 2 * odd * blocks, source)
            counts = (counts[0] + 1 - far, counts[1] + far)
    for begin, number, none in ((0, counts[0], 3 * blocks), (half, counts[1], blocks)):
        for g in range(GROUP - 1):
            entries[0, begin + number + g] = 0
            entries[1, begin + number + g] = 0
            entries[2, begin + number + g] = none
    entries[0, 2 * half - 1] = lax.div(counts[0] + GROUP - 1, GROUP)
    entries[1, 2 * half - 1] = lax.div(counts[1] + GROUP - 1, GROUP)
    entries[2, half - 1] = counts[0]
    entries[2, 2 * half - 1] = counts[1]


def prepare_kernel(total_blocks, place, neighbours, inverse, held, entries, sem):
    copy = pltpu.make_async_copy(inverse, held, sem.at[0])
    copy.start()
    list_entries(place, neighbours, entries, total_blocks)
    copy.wait()


def mix_kernel(levels, place, *refs):
    depth = (len(refs) - 6) // 3
    slabs, sens = refs[:depth], refs[depth : 2 * depth]
    inverse, count, before = refs[2 * depth : 2 * depth + 3]
    parts, (terms, mixed, weighted) = refs[2 * depth + 3 : -3], refs[-3:]
    tracers, cols = slabs[0].shape[1:]
    offset = sens[0].shape[0] - levels
    for s in range(depth):
        weighted[lax.rem(place[0] + depth - s, depth)] = sens[s][offset:]
    terms[...] = before[...]
    for target in range(depth):
        at = lax.rem(target - place[0] + depth, depth)
        for lane in range(0, cols, 128):
            lanes = slice(lane, lane + 128)
            here = pl.ds(pl.multiple_of(place[0] * cols + lane, 128), 128)
            totals = tuple(jnp.zeros((tracers, 128), jnp.float32) for _ in range(levels))
            for s in range(depth):
                base = lax.rem(place[0] + depth - s, depth) * levels

                def add(p, totals, s=s, base=base):
                    value = slabs[s][p, :, lanes].astype(jnp.float32)
                    rows = inverse[base + p, target * levels : (target + 1) * levels, lanes]
                    return tuple(t + rows[q : q + 1] * value for q, t in enumerate(totals))

                totals = lax.fori_loop(0, levels, add, totals, unroll=4)
            wet_levels = count[:, here] - target * levels
            term = jnp.zeros((tracers, 128), jnp.float32)
            for q in range(levels):
                value = totals[q].astype(jnp.bfloat16)
                mixed[at, q, :, lanes] = value
                product = value.astype(jnp.float32) * weighted[target, q, :, lanes].astype(jnp.float32)
                term = term + jnp.where(wet_levels > q, product, 0.0)
            terms[...] += term
    high = terms[...].astype(jnp.bfloat16)
    low = (terms[...] - high.astype(jnp.float32)).astype(jnp.bfloat16)
    for s in range(depth):
        parts[s][:levels] = mixed[s]
        parts[s][levels] = jnp.concatenate([high, low], axis=1)


def gather_kernel(place, *refs):
    slabs, mixed, terms = refs[:-2], refs[-2], refs[-1]
    depth, levels = len(slabs), mixed.shape[1]
    per = slabs[0].shape[2] // 128
    total = jnp.zeros(terms.shape, jnp.float32)
    for s in range(depth):
        origin = lax.rem(place[0] + depth - s, depth)
        for i in range(per):
            mixed[origin * per + i] = slabs[s][:levels, :, i * 128 : (i + 1) * 128]
        behind = slabs[s][levels].astype(jnp.float32)
        total = total + (behind[:, :128] + behind[:, 128:])
    terms[...] = total


def add_entries(entries, start, steps, weights, near, total, ready=None):
    levels = near.shape[1]
    zero = jnp.zeros(near.shape[2:], jnp.bfloat16)
    tracers = zero.shape[0]

    def step(i, _):
        if ready is not None:
            for g in range(GROUP):
                ready(start + i * GROUP + g)
        found = []
        for g in range(GROUP):
            at = start + i * GROUP + g
            entry, block, source = entries[0, at], entries[1, at], entries[2, at]
            for l in range(0, levels, 2):
                lhs = jnp.concatenate([weights[entry, l], weights[entry, l + 1]], axis=1)
                rhs = jnp.concatenate(
                    [
                        jnp.concatenate([near[source, l], zero], axis=1),
                        jnp.concatenate([zero, near[source, l + 1]], axis=1),
                    ],
                    axis=0,
                )
                if g % 2:
                    lhs, rhs = rhs, lhs
                moved = lax.dot_general(
                    lhs, rhs, (((1,), (1,)), ((), ())), preferred_element_type=jnp.float32
                )
                found.append((g, block, l, moved))
        for g, block, l, moved in found:
            moved = moved if g % 2 else moved.T
            total[block, l] += moved[:tracers]
            total[block, l + 1] += moved[tracers:]
        return 0

    lax.fori_loop(0, steps, step, 0)


def near_kernel(load, place, entries, weights, own, mate, state, rates, coupling, *refs):
    if load:
        held, total, near, rates_in, extra, state_in, sem = refs
    else:
        total, near, rates_in, extra = refs
        held, state_in = weights, state
    blocks, levels, tracers, _ = own.shape
    odd = place[1]
    half = entries.shape[1] // 2
    more = [pltpu.make_async_copy(rates, rates_in, extra.at[0])]
    if load:
        more.append(pltpu.make_async_copy(state, state_in, extra.at[1]))
    for copy in more:
        copy.start()

    ready = None
    if load:
        slots = weights.shape[2]

        def fetch(at):
            entry = entries[0, at]
            return pltpu.make_async_copy(
                weights.at[:, lax.div(entry, slots), lax.rem(entry, slots)],
                held.at[entry],
                sem.at[entry],
            )

        def begin(at, _):
            fetch(at).start()
            return 0

        def finish(at, _):
            fetch(at).wait()
            return 0

        lax.fori_loop(0, entries[2, half - 1], begin, 0)
        lax.fori_loop(half, half + entries[2, 2 * half - 1], begin, 0)

        def ready(at):
            @pl.when(at < entries[2, half - 1])
            def _():
                fetch(at).wait()

    near[pl.ds(blocks, blocks)] = own[...]
    near[pl.ds((1 - odd) * 2 * blocks, blocks)] = mate[...]
    near[3 * blocks] = jnp.zeros(near.shape[1:], near.dtype)
    total[...] = jnp.zeros(total.shape, total.dtype)
    add_entries(entries, 0, entries[0, 2 * half - 1], held, near, total, ready)
    for copy in more:
        copy.wait()
    for b in range(blocks):
        lanes = slice(b * 128, (b + 1) * 128)
        values = jnp.concatenate([own[b, l] for l in range(levels)], axis=1)
        both = jnp.dot(coupling[...], values, preferred_element_type=jnp.float32)
        both = both[:tracers] + both[tracers:]
        for l in range(levels):
            source = rates_in[l : l + 1, lanes] * both[:, l * 128 : (l + 1) * 128]
            total[b, l] += source - state_in[l, :, lanes].astype(jnp.float32)
    if load:
        lax.fori_loop(half, half + entries[2, 2 * half - 1], finish, 0)


def far_kernel(place, entries, weights, far, before, count, new, *refs):
    parts, near, total = refs[:-2], refs[-2], refs[-1]
    blocks, levels, tracers, _ = far.shape
    half = entries.shape[1] // 2
    near[pl.ds(0, blocks)] = far[...]
    near[blocks] = jnp.zeros(near.shape[1:], near.dtype)
    total[...] = before[...]
    add_entries(entries, half, entries[1, 2 * half - 1], weights, near, total)
    for b in range(blocks):
        lanes = slice(b * 128, (b + 1) * 128)
        wet_levels = count[:, lanes] - place[0] * levels
        for l in range(levels):
            value = jnp.where(wet_levels > l, total[b, l], 0.0)
            new[l, :, lanes] = value.astype(jnp.bfloat16)
    depth = len(parts)
    for s in range(depth):
        width = parts[s].shape[2]
        start = lax.rem(place[0] + s, depth) * width
        parts[s][...] = new[:, :, pl.ds(pl.multiple_of(start, width), width)]


def ring(count, shift):
    return [(j, (j + shift) % count) for j in range(count)]


def exchange(parts, axis):
    count = len(parts)
    return [parts[0]] + [
        lax.ppermute(parts[s], axis, ring(count, s)) for s in range(1, count)
    ]


def params(mib):
    return pltpu.CompilerParams(vmem_limit_bytes=mib * MIB)


def cost(flops, size):
    return pl.CostEstimate(flops=flops, bytes_accessed=size, transcendentals=0)


def per_device(
    adjoint_seed, transport, neighbours, inv_mix, rates, coupling, sensitivity, depth_count
):
    tracers, levels, cols = adjoint_seed.shape
    blocks, slots = neighbours.shape
    horiz, depth = lax.axis_size("horiz"), lax.axis_size("depth")
    total_blocks = blocks * horiz
    h = lax.axis_index("horiz")
    place = jnp.stack([lax.axis_index("depth"), h % 2, h]).astype(jnp.int32)
    state = jnp.transpose(adjoint_seed, (1, 0, 2))
    sens = jnp.transpose(sensitivity, (1, 0, 2))
    count = depth_count.reshape(1, cols)
    mixing = coupling.T
    high = lax.reduce_precision(mixing, 8, 7)
    pair = jnp.concatenate([high, mixing - high], axis=0).astype(jnp.bfloat16)

    width = cols // depth
    block_shape = (blocks, levels, tracers, 128)
    terms_shape = jax.ShapeDtypeStruct((tracers, 128), jnp.float32)
    swap = [(i, i ^ 1) for i in range(horiz)]
    cross = []
    for i in range(1, horiz, 2):
        cross += [(i, (i + 1) % horiz), ((i + 1) % horiz, i)]

    def keep(value):
        return pltpu.with_memory_space_constraint(value, pltpu.VMEM)

    def leave(value):
        return pltpu.with_memory_space_constraint(value, pltpu.HBM)

    parts = pl.pallas_call(
        split_kernel,
        out_shape=[jax.ShapeDtypeStruct((2 * levels, tracers, width), jnp.bfloat16)] * depth,
        in_specs=[SMEM, HBM, HBM],
        out_specs=[VMEM] * depth,
        scratch_shapes=[pltpu.SemaphoreType.DMA((2 * depth,))],
        compiler_params=params(4),
        name="split",
    )(place, leave(state), leave(sens))
    slabs = exchange(parts, "depth")
    sens_slabs = slabs
    inverse, entries = pl.pallas_call(
        functools.partial(prepare_kernel, total_blocks),
        out_shape=[
            pltpu.VMEM(inv_mix.shape, jnp.float32),
            jax.ShapeDtypeStruct((3, 128), jnp.int32),
        ],
        in_specs=[SMEM, SMEM, HBM],
        out_specs=[VMEM, SMEM],
        scratch_shapes=[pltpu.SemaphoreType.DMA((1,))],
        compiler_params=params(4),
        name="prepare",
    )(place, neighbours, leave(inv_mix))
    results = []
    terms = jnp.zeros((tracers, 128), jnp.float32)
    held = None
    for step in range(2):
        last = step == 1
        *parts, terms = pl.pallas_call(
            functools.partial(mix_kernel, levels),
            out_shape=[jax.ShapeDtypeStruct((levels + 1, tracers, width), jnp.bfloat16)] * depth
            + [terms_shape],
            in_specs=[SMEM] + [VMEM] * (2 * depth + 3),
            out_specs=[VMEM] * (depth + 1),
            scratch_shapes=[pltpu.VMEM((depth, levels, tracers, width), jnp.bfloat16)] * 2,
            compiler_params=params(4),
            name="mix",
        )(place, *slabs, *sens_slabs, keep(inverse), count, terms)
        slabs = exchange(parts, "depth")
        own, total_terms = pl.pallas_call(
            gather_kernel,
            out_shape=[jax.ShapeDtypeStruct(block_shape, jnp.bfloat16), terms_shape],
            in_specs=[SMEM] + [VMEM] * depth,
            out_specs=[VMEM] * 2,
            compiler_params=params(4),
            name="gather",
        )(place, *slabs)
        mate = lax.ppermute(own, "horiz", swap)
        far = lax.ppermute(own, "horiz", cross)
        total_shape = jax.ShapeDtypeStruct(block_shape, jnp.float32)
        scratch = [
            pltpu.VMEM((3 * blocks + 1,) + block_shape[1:], jnp.bfloat16),
            pltpu.VMEM((levels, cols), jnp.float32),
            pltpu.SemaphoreType.DMA((2,)),
        ]
        if not last:
            held, total = pl.pallas_call(
                functools.partial(near_kernel, True),
                out_shape=[
                    pltpu.VMEM((blocks * slots, levels, 128, 128), jnp.bfloat16),
                    total_shape,
                ],
                in_specs=[SMEM, SMEM, HBM, VMEM, VMEM, HBM, HBM, VMEM],
                out_specs=[VMEM, VMEM],
                scratch_shapes=scratch
                + [
                    pltpu.VMEM((levels, tracers, cols), jnp.bfloat16),
                    pltpu.SemaphoreType.DMA((blocks * slots,)),
                ],
                compiler_params=params(4),
                cost_estimate=cost(0, 16 * MIB),
                name="near_load",
            )(place, entries, leave(transport), own, mate, leave(state), leave(rates), pair)
        else:
            total = pl.pallas_call(
                functools.partial(near_kernel, False),
                out_shape=total_shape,
                in_specs=[SMEM, SMEM, VMEM, VMEM, VMEM, VMEM, HBM, VMEM],
                out_specs=VMEM,
                scratch_shapes=scratch,
                compiler_params=params(4),
                cost_estimate=cost(0, 16 * MIB),
                name="near",
            )(place, entries, keep(held), own, mate, state, leave(rates), pair)
        whole = jax.ShapeDtypeStruct((levels, tracers, cols), jnp.bfloat16)
        slab = jax.ShapeDtypeStruct((levels, tracers, width), jnp.bfloat16)
        state, *parts = pl.pallas_call(
            far_kernel,
            out_shape=[whole] + ([] if last else [slab] * depth),
            in_specs=[SMEM] * 2 + [VMEM] * 4,
            out_specs=[VMEM] * (1 if last else depth + 1),
            scratch_shapes=[
                pltpu.VMEM((blocks + 1,) + block_shape[1:], jnp.bfloat16),
                pltpu.VMEM(block_shape, jnp.float32),
            ],
            compiler_params=params(4),
            name="far",
        )(place, entries, keep(held), far, total, count)
        results.append(jnp.transpose(state, (1, 0, 2)))
        if not last:
            slabs = exchange(parts, "depth")
    terms = total_terms
    for flip in (1, 3, 7, 9, 25):
        if flip == 7:
            terms, _ = lax.optimization_barrier((terms, total))
        terms = terms + lax.ppermute(terms, "horiz", [(i, i ^ flip) for i in range(horiz)])
    gradient = jnp.sum(terms, axis=1) / math.sqrt(levels * depth * total_blocks * 128)
    return (results[0], results[1], gradient)


def solution(mesh):
    return jax.shard_map(
        per_device,
        mesh=mesh,
        in_specs=(
            P(None, "depth", "horiz"),
            P("depth", "horiz", None, None, None),
            P("horiz", None),
            P(None, None, ("horiz", "depth")),
            P("depth", "horiz"),
            P(),
            P(None, "depth", "horiz"),
            P("horiz"),
        ),
        out_specs=(P(None, "depth", "horiz"), P(None, "depth", "horiz"), P()),
        check_vma=False,
    )
```

```python
import functools
import math

import jax
import jax.numpy as jnp
from jax import lax
from jax.experimental import pallas as pl
from jax.experimental.pallas import tpu as pltpu
from jax.sharding import PartitionSpec as P

VMEM = pl.BlockSpec(memory_space=pltpu.VMEM)
SMEM = pl.BlockSpec(memory_space=pltpu.SMEM)
HBM = pl.BlockSpec(memory_space=pltpu.HBM)
MIB = 1024 * 1024
GROUP = 4


def split_kernel(place, state, sens, *refs):
    one, two, three, own, own_sens, later, held, sem = refs
    levels, _, width = own.shape
    depth = state.shape[2] // width
    copies = [
        pltpu.make_async_copy(whole, held.at[i], sem.at[i])
        for i, whole in enumerate((state, sens))
    ]
    for copy in copies:
        copy.start()
    for i, targets in enumerate(
        (
            ((own, 0, 0), (one, 0, 1), (two, 0, 2), (three, 0, 3)),
            ((own_sens, 0, 0), (one, 1, 1), (later, 0, 2), (three, 1, 3)),
        )
    ):
        copies[i].wait()
        for part, at, s in targets:
            start = lax.rem(place[0] + s, depth) * width
            part[at * levels : (at + 1) * levels] = held[
                i, :, :, pl.ds(pl.multiple_of(start, width), width)
            ]


def list_entries(place, neighbours, entries, total_blocks):
    blocks, slots = neighbours.shape
    half = entries.shape[1] // 2
    odd = place[1]
    shift = 2 * blocks * odd
    counts = (jnp.int32(0), jnp.int32(0))
    for b in range(blocks):
        row = place[2] * blocks + (b - blocks)
        for k in range(slots):
            ahead = neighbours[b, k] - row
            ahead = jnp.where(ahead < 0, ahead + total_blocks, ahead)
            ahead = jnp.where(ahead >= total_blocks, ahead - total_blocks, ahead)
            source = b + jnp.clip(ahead, 0, 2 * blocks)
            inside = source - shift
            far = jnp.where((inside >= 0) & (inside < blocks), 1, 0)
            at = jnp.where(far == 1, half + counts[1], counts[0])
            entries[0, at] = b * slots + k
            entries[1, at] = b
            entries[2, at] = jnp.where(far == 1, inside, source)
            counts = (counts[0] + 1 - far, counts[1] + far)
    for begin, number, none in ((0, counts[0], 3 * blocks), (half, counts[1], blocks)):
        for g in range(GROUP - 1):
            entries[0, begin + number + g] = 0
            entries[1, begin + number + g] = 0
            entries[2, begin + number + g] = none
    entries[0, 2 * half - 1] = lax.div(counts[0] + GROUP - 1, GROUP)
    entries[1, 2 * half - 1] = lax.div(counts[1] + GROUP - 1, GROUP)
    entries[2, half - 1] = counts[0]
    entries[2, 2 * half - 1] = counts[1]


def prepare_kernel(inverse, held, sem):
    copy = pltpu.make_async_copy(inverse, held, sem.at[0])
    copy.start()
    copy.wait()


def list_kernel(total_blocks, place, neighbours, pair, count, entries, pair_out, count_out):
    pair_out[...] = pair[...]
    count_out[...] = count[...]
    list_entries(place, neighbours, entries, total_blocks)


def add_products(place, slabs, steps, inverse, totals, target, lanes, levels):
    depth = inverse.shape[0] // levels
    for slab, s in zip(slabs, steps):
        base = lax.rem(place[0] + depth - s, depth) * levels

        def add(p, totals):
            value = slab[p, :, lanes].astype(jnp.float32)
            rows = inverse[base + p, target * levels : (target + 1) * levels, lanes]
            return tuple(t + rows[q : q + 1] * value for q, t in enumerate(totals))

        totals = lax.fori_loop(0, levels, add, totals, unroll=levels)
    return totals


def early_kernel(place, slab, inverse, partial):
    levels, tracers, cols = slab.shape
    for target in range(inverse.shape[0] // levels):
        for lane in range(0, cols, 128):
            lanes = slice(lane, lane + 128)
            totals = tuple(jnp.zeros((tracers, 128), jnp.float32) for _ in range(levels))
            totals = add_products(place, [slab], [0], inverse, totals, target, lanes, levels)
            for q in range(levels):
                partial[target, q, :, lanes] = totals[q]


def weigh(place, pairs, count):
    total = None
    for s, mixed, sens in pairs:
        levels, _, cols = pairs[0][2].shape
        depth = count.shape[1] // cols
        offset = sens.shape[0] - levels
        target = lax.rem(place[0] + depth - s, depth)
        for lane in range(0, cols, 128):
            lanes = slice(lane, lane + 128)
            here = pl.ds(pl.multiple_of(place[0] * cols + lane, 128), 128)
            wet_levels = count[:, here] - target * levels
            for q in range(levels):
                value = sum(part[q, :, lanes].astype(jnp.float32) for part in mixed)
                product = value * sens[offset + q, :, lanes].astype(jnp.float32)
                product = jnp.where(wet_levels > q, product, 0.0)
                total = product if total is None else total + product
    return total


def weigh_kernel(place, *refs):
    own, one, three, own_sens, one_sens, three_sens, count, terms = refs
    pairs = ((0, [own], own_sens), (1, [three], one_sens), (3, [one], three_sens))
    terms[...] = weigh(place, pairs, count)


def mix_kernel(number, place, *refs):
    mixed = refs[-1]
    depth, levels, tracers, cols = mixed.shape
    slabs, inverse, partial = refs[: depth - 1], refs[depth - 1], refs[depth]
    parts = refs[-1 - depth : -1]
    for target in range(depth):
        at = lax.rem(target - place[0] + depth, depth)
        for lane in range(0, cols, 128):
            lanes = slice(lane, lane + 128)
            totals = tuple(partial[target, q, :, lanes] for q in range(levels))
            totals = add_products(
                place, slabs, range(1, depth), inverse, totals, target, lanes, levels
            )
            for q in range(levels):
                mixed[at, q, :, lanes] = totals[q].astype(jnp.bfloat16)
    for s in range(depth):
        parts[s][:levels] = mixed[s]
    if number:
        parts[depth - 1][levels:] = refs[depth + 1][...]


def mix_last_kernel(place, *refs):
    mixed = refs[-1]
    depth, levels = mixed.shape[:2]
    own_sens, one_sens, three_sens, early_mixed, count, before = refs[depth + 1 : depth + 7]
    parts = refs[-1 - depth : -1]
    mix_kernel(0, place, *refs[: depth + 1], *parts, mixed)
    pairs = (
        (0, [mixed.at[0]], own_sens),
        (1, [mixed.at[3]], one_sens),
        (2, [mixed.at[2], early_mixed], refs[2]),
        (3, [mixed.at[1]], three_sens),
    )
    terms = before[...] + weigh(place, pairs, count)
    high = terms.astype(jnp.bfloat16)
    low = (terms - high.astype(jnp.float32)).astype(jnp.bfloat16)
    for s in range(depth):
        parts[s][levels] = jnp.concatenate([high, low], axis=1)


def gather_kernel(depth, scale, place, *refs):
    slabs, mixed = refs[:depth], refs[depth]
    levels = mixed.shape[1]
    per = slabs[0].shape[2] // 128
    for s in range(depth):
        origin = lax.rem(place[0] + depth - s, depth)
        for i in range(per):
            mixed[origin * per + i] = slabs[s][:levels, :, i * 128 : (i + 1) * 128]
    if len(refs) > depth + 1:
        terms, message = refs[depth + 1 :]
        total = jnp.zeros(terms.shape, jnp.float32)
        for s in range(depth):
            behind = slabs[s][levels].astype(jnp.float32)
            total = total + (behind[:, :128] + behind[:, 128:])
        total = jnp.broadcast_to(jnp.sum(total, axis=1, keepdims=True), terms.shape) * scale
        terms[...] = total
        high = total.astype(jnp.bfloat16)
        blocks = mixed.shape[0]
        message[:blocks] = mixed[...]
        message[blocks, 0] = high
        message[blocks, 1] = (total - high.astype(jnp.float32)).astype(jnp.bfloat16)
        for l in range(2, levels):
            message[blocks, l] = jnp.zeros_like(high)


def add_entries(entries, start, steps, weights, near, total, ready=None):
    levels = near.shape[1]
    zero = jnp.zeros(near.shape[2:], jnp.bfloat16)
    tracers = zero.shape[0]

    def step(i, _):
        if ready is not None:
            for g in range(GROUP):
                ready(start + i * GROUP + g)
        found = []
        for g in range(GROUP):
            at = start + i * GROUP + g
            entry, block, source = entries[0, at], entries[1, at], entries[2, at]
            for l in range(0, levels, 2):
                lhs = jnp.concatenate([weights[entry, l], weights[entry, l + 1]], axis=1)
                rhs = jnp.concatenate(
                    [
                        jnp.concatenate([near[source, l], zero], axis=1),
                        jnp.concatenate([zero, near[source, l + 1]], axis=1),
                    ],
                    axis=0,
                )
                if g % 2:
                    lhs, rhs = rhs, lhs
                moved = lax.dot_general(
                    lhs, rhs, (((1,), (1,)), ((), ())), preferred_element_type=jnp.float32
                )
                found.append((g, block, l, moved))
        for g, block, l, moved in found:
            moved = moved if g % 2 else moved.T
            total[block, l] += moved[:tracers]
            total[block, l + 1] += moved[tracers:]
        return 0

    lax.fori_loop(0, steps, step, 0)


def near_kernel(load, place, entries, weights, own, mate, state, rates, coupling, *refs):
    if load:
        held, total, near, rates_in, state_in, extra, sem = refs
    else:
        total, near, rates_in, state_in, extra = refs
        held = weights
    blocks, levels, tracers, _ = own.shape
    odd = place[1]
    half = entries.shape[1] // 2
    more = [
        pltpu.make_async_copy(rates, rates_in, extra.at[0]),
        pltpu.make_async_copy(state, state_in, extra.at[1]),
    ]
    for copy in more:
        copy.start()

    ready = None
    if load:
        slots = weights.shape[2]

        def fetch(at):
            entry, block = entries[0, at], entries[1, at]
            return pltpu.make_async_copy(
                weights.at[:, block, entry - block * slots],
                held.at[entry],
                sem.at[entry],
            )

        def begin(at, _):
            fetch(at).start()
            return 0

        def finish(at, _):
            fetch(at).wait()
            return 0

        lax.fori_loop(0, entries[2, half - 1], begin, 0)
        lax.fori_loop(half, half + entries[2, 2 * half - 1], begin, 0)

        def ready(at):
            @pl.when(at < entries[2, half - 1])
            def _():
                fetch(at).wait()

    near[pl.ds(blocks, blocks)] = own[...]
    near[pl.ds((1 - odd) * 2 * blocks, blocks)] = mate[:blocks]
    near[3 * blocks] = jnp.zeros(near.shape[1:], near.dtype)

    def add_source():
        for copy in more:
            copy.wait()
        for b in range(blocks):
            lanes = slice(b * 128, (b + 1) * 128)
            values = jnp.concatenate([own[b, l] for l in range(levels)], axis=1)
            both = lax.dot_general(
                coupling[...], values, (((0,), (0,)), ((), ())), preferred_element_type=jnp.float32
            )
            both = both[:tracers] + both[tracers:]
            for l in range(levels):
                source = rates_in[l : l + 1, lanes] * both[:, l * 128 : (l + 1) * 128]
                total[b, l] += source - state_in[l, :, lanes].astype(jnp.float32)

    total[...] = jnp.zeros(total.shape, total.dtype)
    if load:
        add_source()
    steps = entries[0, 2 * half - 1]
    if not load:
        steps = lax.div(steps, 2)
    add_entries(entries, 0, steps, held, near, total, ready)
    if not load:
        add_source()
    if load:
        lax.fori_loop(half, half + entries[2, 2 * half - 1], finish, 0)


def rest_kernel(place, entries, weights, own, mate, before, total, near):
    blocks = own.shape[0]
    half = entries.shape[1] // 2
    near[pl.ds(blocks, blocks)] = own[...]
    near[pl.ds((1 - place[1]) * 2 * blocks, blocks)] = mate[:blocks]
    near[3 * blocks] = jnp.zeros(near.shape[1:], near.dtype)
    total[...] = before[...]
    steps = entries[0, 2 * half - 1]
    done = lax.div(steps, 2)
    add_entries(entries, done * GROUP, steps - done, weights, near, total)


def far_kernel(more, place, entries, weights, far, before, count, *refs):
    behind, new, parts, (near, total) = refs[:more], refs[more], refs[more + 1 : -2], refs[-2:]
    blocks, levels, tracers, _ = far.shape
    half = entries.shape[1] // 2
    near[pl.ds(0, blocks)] = far[...]
    near[blocks] = jnp.zeros(near.shape[1:], near.dtype)
    total[...] = before[...]
    add_entries(entries, half, entries[1, 2 * half - 1], weights, near, total)
    for b in range(blocks):
        lanes = slice(b * 128, (b + 1) * 128)
        wet_levels = count[:, lanes] - place[0] * levels
        for l in range(levels):
            value = jnp.where(wet_levels > l, total[b, l], 0.0)
            new[l, :, lanes] = value.astype(jnp.bfloat16)
    depth = len(parts)
    for s in range(depth):
        width = parts[s].shape[2]
        start = lax.rem(place[0] + s, depth) * width
        parts[s][:levels] = new[:, :, pl.ds(pl.multiple_of(start, width), width)]
    for passed_on in behind:
        parts[depth - 1][levels:] = passed_on[levels:]


def ring(count, shift):
    return [(j, (j + shift) % count) for j in range(count)]


def exchange(parts, axis):
    count = len(parts)
    return [parts[0]] + [
        lax.ppermute(parts[s], axis, ring(count, s)) for s in range(1, count)
    ]


def params(mib):
    return pltpu.CompilerParams(vmem_limit_bytes=mib * MIB)


def cost(flops, size):
    return pl.CostEstimate(flops=flops, bytes_accessed=size, transcendentals=0)


def per_device(
    adjoint_seed, transport, neighbours, inv_mix, rates, coupling, sensitivity, depth_count
):
    tracers, levels, cols = adjoint_seed.shape
    blocks, slots = neighbours.shape
    horiz, depth = lax.axis_size("horiz"), lax.axis_size("depth")
    total_blocks = blocks * horiz
    h = lax.axis_index("horiz")
    place = jnp.stack([lax.axis_index("depth"), h % 2, h]).astype(jnp.int32)
    state = jnp.transpose(adjoint_seed, (1, 0, 2))
    sens = jnp.transpose(sensitivity, (1, 0, 2))
    count = depth_count.reshape(1, cols)
    high = lax.reduce_precision(coupling, 8, 7)
    pair = jnp.concatenate([high, coupling - high], axis=1).astype(jnp.bfloat16)
    scale = 1.0 / math.sqrt(levels * depth * total_blocks * 128)

    width = cols // depth
    block_shape = (blocks, levels, tracers, 128)
    terms_shape = jax.ShapeDtypeStruct((tracers, 128), jnp.float32)
    swap = [(i, i ^ 1) for i in range(horiz)]
    cross = []
    for i in range(1, horiz, 2):
        cross += [(i, (i + 1) % horiz), ((i + 1) % horiz, i)]

    def keep(value):
        return pltpu.with_memory_space_constraint(value, pltpu.VMEM)

    def leave(value):
        return pltpu.with_memory_space_constraint(value, pltpu.HBM)

    whole = jax.ShapeDtypeStruct((levels, tracers, cols), jnp.bfloat16)
    slab = jax.ShapeDtypeStruct((levels, tracers, width), jnp.bfloat16)
    longer = jax.ShapeDtypeStruct((levels + 1, tracers, width), jnp.bfloat16)
    total_shape = jax.ShapeDtypeStruct(block_shape, jnp.float32)
    partial_shape = jax.ShapeDtypeStruct((depth, levels, tracers, width), jnp.float32)
    mixed_scratch = pltpu.VMEM((depth, levels, tracers, width), jnp.bfloat16)

    def several(number):
        return jax.ShapeDtypeStruct((number * levels, tracers, width), jnp.bfloat16)

    *messages, own_state, own_sens, later_sens = pl.pallas_call(
        split_kernel,
        out_shape=[several(number) for number in (2, 1, 2, 1, 1, 1)],
        in_specs=[SMEM, HBM, HBM],
        out_specs=[VMEM] * 6,
        scratch_shapes=[
            pltpu.VMEM((2,) + whole.shape, jnp.bfloat16),
            pltpu.SemaphoreType.DMA((2,)),
        ],
        compiler_params=params(8),
        name="split",
    )(place, leave(state), leave(sens))
    slabs = exchange([own_state] + messages, "depth")
    inverse = pl.pallas_call(
        prepare_kernel,
        out_shape=pltpu.VMEM(inv_mix.shape, jnp.float32),
        in_specs=[HBM],
        out_specs=VMEM,
        scratch_shapes=[pltpu.SemaphoreType.DMA((1,))],
        compiler_params=params(4),
        name="prepare",
    )(leave(inv_mix))

    def early(slab):
        return pl.pallas_call(
            early_kernel,
            out_shape=partial_shape,
            in_specs=[SMEM] + [VMEM] * 2,
            out_specs=VMEM,
            compiler_params=params(4),
            cost_estimate=cost(0, 3 * MIB),
            name="early",
        )(place, slab, keep(inverse))

    def gather(slabs, shapes):
        return pl.pallas_call(
            functools.partial(gather_kernel, depth, scale),
            out_shape=shapes,
            in_specs=[SMEM] + [VMEM] * depth,
            out_specs=[VMEM] * len(shapes),
            compiler_params=params(4),
            name="gather",
        )(place, *slabs)

    def move_far(far, total, shapes, *behind):
        return pl.pallas_call(
            functools.partial(far_kernel, len(behind)),
            out_shape=shapes,
            in_specs=[SMEM] * 2 + [VMEM] * (4 + len(behind)),
            out_specs=[VMEM] * len(shapes),
            scratch_shapes=[
                pltpu.VMEM((blocks + 1,) + block_shape[1:], jnp.bfloat16),
                pltpu.VMEM(block_shape, jnp.float32),
            ],
            compiler_params=params(4),
            cost_estimate=cost(0, 8 * MIB),
            name="far",
        )(place, entries, keep(held), keep(far), keep(total), keep(count), *behind)

    near_scratch = pltpu.VMEM((3 * blocks + 1,) + block_shape[1:], jnp.bfloat16)
    scratch = [
        near_scratch,
        pltpu.VMEM((levels, cols), jnp.float32),
        pltpu.VMEM((levels, tracers, cols), jnp.bfloat16),
        pltpu.SemaphoreType.DMA((2,)),
    ]
    block_array = jax.ShapeDtypeStruct(block_shape, jnp.bfloat16)

    partial = early(slabs[0])
    one_sens, three_sens = slabs[1], slabs[3]
    mixed = pl.pallas_call(
        functools.partial(mix_kernel, 1),
        out_shape=[slab] * (depth - 1) + [several(2)],
        in_specs=[SMEM] + [VMEM] * (depth + 2),
        out_specs=[VMEM] * depth,
        scratch_shapes=[mixed_scratch],
        compiler_params=params(4),
        name="mix",
    )(place, *slabs[1:], keep(inverse), keep(partial), later_sens)
    slabs = exchange(mixed, "depth")
    pair, neighbours, _ = lax.optimization_barrier((pair, neighbours, mixed))
    entries, pair, count = pl.pallas_call(
        functools.partial(list_kernel, total_blocks),
        out_shape=[
            jax.ShapeDtypeStruct((3, 128), jnp.int32),
            jax.ShapeDtypeStruct(pair.shape, pair.dtype),
            jax.ShapeDtypeStruct(count.shape, count.dtype),
        ],
        in_specs=[SMEM, SMEM, VMEM, VMEM],
        out_specs=[SMEM, VMEM, VMEM],
        compiler_params=params(4),
        name="list",
    )(place, neighbours, pair, count)
    slabs, entries, pair = lax.optimization_barrier((slabs, entries, pair))
    (own,) = gather(slabs, [block_array])
    mate = lax.ppermute(own, "horiz", swap)
    far = lax.ppermute(own, "horiz", cross)
    held, total = pl.pallas_call(
        functools.partial(near_kernel, True),
        out_shape=[
            pltpu.VMEM((blocks * slots, levels, 128, 128), jnp.bfloat16),
            total_shape,
        ],
        in_specs=[SMEM, SMEM, HBM, VMEM, VMEM, HBM, HBM, VMEM],
        out_specs=[VMEM, VMEM],
        scratch_shapes=scratch + [pltpu.SemaphoreType.DMA((blocks * slots,))],
        compiler_params=params(4),
        cost_estimate=cost(0, 16 * MIB),
        name="near_load",
    )(place, entries, leave(transport), keep(own), keep(mate), leave(state), leave(rates), pair)
    shapes = [whole] + [slab] * (depth - 1) + [several(2)]
    first, *parts = move_far(far, total, shapes, slabs[3])

    slabs = exchange(parts, "depth")
    partial = early(slabs[0])
    terms = pl.pallas_call(
        weigh_kernel,
        out_shape=terms_shape,
        in_specs=[SMEM] + [VMEM] * 7,
        out_specs=VMEM,
        compiler_params=params(4),
        name="weigh",
    )(place, mixed[0], mixed[1], mixed[3], own_sens, one_sens, three_sens, count)
    parts = pl.pallas_call(
        mix_last_kernel,
        out_shape=[longer] * depth,
        in_specs=[SMEM] + [VMEM] * (depth + 7),
        out_specs=[VMEM] * depth,
        scratch_shapes=[mixed_scratch],
        compiler_params=params(4),
        name="mix_last",
    )(
        place, *slabs[1:], keep(inverse), keep(partial),
        own_sens, one_sens, three_sens, mixed[2], keep(count), terms,
    )
    slabs = exchange(parts, "depth")
    message_shape = jax.ShapeDtypeStruct((blocks + 1,) + block_shape[1:], jnp.bfloat16)
    own, terms, message = gather(slabs, [block_array, terms_shape, message_shape])
    mate = lax.ppermute(message, "horiz", swap)
    far = lax.ppermute(own, "horiz", cross)

    def add_pairs(terms, flip):
        return terms + lax.ppermute(terms, "horiz", [(i, i ^ flip) for i in range(horiz)])

    terms = terms + (mate[blocks, 0].astype(jnp.float32) + mate[blocks, 1].astype(jnp.float32))
    terms, own, mate = lax.optimization_barrier((terms, own, mate))
    total = pl.pallas_call(
        functools.partial(near_kernel, False),
        out_shape=total_shape,
        in_specs=[SMEM, SMEM, VMEM, VMEM, VMEM, HBM, HBM, VMEM],
        out_specs=VMEM,
        scratch_shapes=scratch,
        compiler_params=params(4),
        cost_estimate=cost(0, 10 * MIB),
        name="near",
    )(place, entries, keep(held), keep(own), keep(mate), leave(first), leave(rates), pair)
    terms = add_pairs(terms, 7)
    terms, total = lax.optimization_barrier((terms, total))
    total = pl.pallas_call(
        rest_kernel,
        out_shape=total_shape,
        in_specs=[SMEM, SMEM] + [VMEM] * 4,
        out_specs=VMEM,
        scratch_shapes=[near_scratch],
        compiler_params=params(4),
        cost_estimate=cost(0, 10 * MIB),
        name="rest",
    )(place, entries, keep(held), keep(own), keep(mate), keep(total))
    terms = add_pairs(terms, 25)
    terms, total = lax.optimization_barrier((terms, total))
    (second,) = move_far(far, total, [whole])
    terms = add_pairs(terms, 9)
    terms, second = lax.optimization_barrier((terms, second))
    terms = add_pairs(terms, 3)
    gradient = terms[:, 0]
    return (jnp.transpose(first, (1, 0, 2)), jnp.transpose(second, (1, 0, 2)), gradient)


def solution(mesh):
    return jax.shard_map(
        per_device,
        mesh=mesh,
        in_specs=(
            P(None, "depth", "horiz"),
            P("depth", "horiz", None, None, None),
            P("horiz", None),
            P(None, None, ("horiz", "depth")),
            P("depth", "horiz"),
            P(),
            P(None, "depth", "horiz"),
            P("horiz"),
        ),
        out_specs=(P(None, "depth", "horiz"), P(None, "depth", "horiz"), P()),
        check_vma=False,
    )
```

```python
import functools
import math

import jax
import jax.numpy as jnp
from jax import lax
from jax.experimental import pallas as pl
from jax.experimental.pallas import tpu as pltpu
from jax.sharding import PartitionSpec as P

VMEM = pl.BlockSpec(memory_space=pltpu.VMEM)
SMEM = pl.BlockSpec(memory_space=pltpu.SMEM)
HBM = pl.BlockSpec(memory_space=pltpu.HBM)
MIB = 1024 * 1024
AHEAD = 3
GROUP = 4


def split_kernel(place, state, sens, *refs):
    one, two, three, own, own_sens, later_one, later_two, kept, held, sem = refs
    levels, _, width = own.shape
    depth = state.shape[2] // width
    copies = [
        pltpu.make_async_copy(state, kept, sem.at[0]),
        pltpu.make_async_copy(sens, held, sem.at[1]),
    ]
    for copy in copies:
        copy.start()
    for i, targets in enumerate(
        (
            ((own, 0, 0), (one, 0, 1), (two, 0, 2), (three, 0, 3)),
            ((own_sens, 0, 0), (later_one, 0, 1), (later_two, 0, 2), (three, 1, 3)),
        )
    ):
        copies[i].wait()
        for part, at, s in targets:
            start = lax.rem(place[0] + s, depth) * width
            whole = (kept, held)[i]
            part[at * levels : (at + 1) * levels] = whole[
                :, :, pl.ds(pl.multiple_of(start, width), width)
            ]


def list_entries(place, neighbours, entries, total_blocks):
    blocks, slots = neighbours.shape
    half = entries.shape[1] // 2
    odd = place[1]
    shift = 2 * blocks * odd
    counts = (jnp.int32(0), jnp.int32(0))
    for b in range(blocks):
        row = place[2] * blocks + (b - blocks)
        for k in range(slots):
            ahead = neighbours[b, k] - row
            ahead = jnp.where(ahead < 0, ahead + total_blocks, ahead)
            ahead = jnp.where(ahead >= total_blocks, ahead - total_blocks, ahead)
            source = b + jnp.clip(ahead, 0, 2 * blocks)
            inside = source - shift
            far = jnp.where((inside >= 0) & (inside < blocks), 1, 0)
            at = jnp.where(far == 1, half + counts[1], counts[0])
            entries[0, at] = k
            entries[1, at] = b
            entries[2, at] = jnp.where(far == 1, inside, source)
            counts = (counts[0] + 1 - far, counts[1] + far)
    for begin, number, none in ((0, counts[0], 3 * blocks), (half, counts[1], blocks)):
        for g in range(GROUP - 1):
            entries[0, begin + number + g] = 0
            entries[1, begin + number + g] = 0
            entries[2, begin + number + g] = none
    entries[0, 2 * half - 1] = lax.div(counts[0] + GROUP - 1, GROUP)
    entries[1, 2 * half - 1] = lax.div(counts[1] + GROUP - 1, GROUP)
    entries[2, half - 1] = counts[0]
    entries[2, 2 * half - 1] = counts[1]


def prepare_kernel(inverse, rates, weights, held, held_rates, held_weights, sem):
    copies = [
        pltpu.make_async_copy(inverse, held, sem.at[0]),
        pltpu.make_async_copy(rates, held_rates, sem.at[1]),
    ]
    for b in range(AHEAD):
        copies.append(pltpu.make_async_copy(weights.at[:, b], held_weights.at[b], sem.at[2 + b]))
    for copy in copies:
        copy.start()
    for copy in copies:
        copy.wait()


def list_kernel(total_blocks, place, neighbours, coupling, count, entries, pair, count_out):
    high = coupling[...].astype(jnp.bfloat16)
    low = (coupling[...] - high.astype(jnp.float32)).astype(jnp.bfloat16)
    pair[...] = jnp.concatenate([high, low], axis=1)
    count_out[...] = count[...]
    list_entries(place, neighbours, entries, total_blocks)


def add_products(place, slabs, steps, inverse, totals, target, lanes, levels):
    depth = inverse.shape[0] // levels
    for slab, s in zip(slabs, steps):
        base = lax.rem(place[0] + depth - s, depth) * levels

        def add(p, totals):
            value = slab[p, :, lanes].astype(jnp.float32)
            rows = inverse[base + p, target * levels : (target + 1) * levels, lanes]
            return tuple(t + rows[q : q + 1] * value for q, t in enumerate(totals))

        totals = lax.fori_loop(0, levels, add, totals, unroll=levels)
    return totals


def early_kernel(place, slab, inverse, partial):
    levels, tracers, cols = slab.shape
    for target in range(inverse.shape[0] // levels):
        for lane in range(0, cols, 128):
            lanes = slice(lane, lane + 128)
            totals = tuple(jnp.zeros((tracers, 128), jnp.float32) for _ in range(levels))
            totals = add_products(place, [slab], [0], inverse, totals, target, lanes, levels)
            for q in range(levels):
                partial[target, q, :, lanes] = totals[q]


def weigh(place, pairs, count):
    total = None
    for s, mixed, sens in pairs:
        levels, _, cols = pairs[0][2].shape
        depth = count.shape[1] // cols
        offset = sens.shape[0] - levels
        target = lax.rem(place[0] + depth - s, depth)
        for lane in range(0, cols, 128):
            lanes = slice(lane, lane + 128)
            here = pl.ds(pl.multiple_of(place[0] * cols + lane, 128), 128)
            wet_levels = count[:, here] - target * levels
            for q in range(levels):
                value = sum(part[q, :, lanes].astype(jnp.float32) for part in mixed)
                product = value * sens[offset + q, :, lanes].astype(jnp.float32)
                product = jnp.where(wet_levels > q, product, 0.0)
                total = product if total is None else total + product
    return total


def weigh_kernel(place, *refs):
    own, one, three, own_sens, one_sens, three_sens, count, terms = refs
    pairs = ((0, [own], own_sens), (1, [three], one_sens), (3, [one], three_sens))
    terms[...] = weigh(place, pairs, count)


def mix_kernel(number, place, *refs):
    mixed = refs[-1]
    depth, levels, tracers, cols = mixed.shape
    slabs, inverse, partial = refs[: depth - 1], refs[depth - 1], refs[depth]
    parts = refs[-1 - depth : -1]
    for target in range(depth):
        at = lax.rem(target - place[0] + depth, depth)
        for lane in range(0, cols, 128):
            lanes = slice(lane, lane + 128)
            totals = tuple(partial[target, q, :, lanes] for q in range(levels))
            totals = add_products(
                place, slabs, range(1, depth), inverse, totals, target, lanes, levels
            )
            for q in range(levels):
                mixed[at, q, :, lanes] = totals[q].astype(jnp.bfloat16)
    for s in range(depth):
        parts[s][:levels] = mixed[s]
    for i in range(number):
        parts[2 * i + 1][levels:] = refs[depth + 1 + i][...]


def mix_last_kernel(place, *refs):
    mixed = refs[-1]
    depth, levels = mixed.shape[:2]
    own_sens, one_sens, three_sens, early_mixed, count, before = refs[depth + 1 : depth + 7]
    parts = refs[-1 - depth : -1]
    mix_kernel(0, place, *refs[: depth + 1], *parts, mixed)
    pairs = (
        (0, [mixed.at[0]], own_sens),
        (1, [mixed.at[3]], one_sens),
        (2, [mixed.at[2], early_mixed], refs[2]),
        (3, [mixed.at[1]], three_sens),
    )
    terms = before[...] + weigh(place, pairs, count)
    high = terms.astype(jnp.bfloat16)
    low = (terms - high.astype(jnp.float32)).astype(jnp.bfloat16)
    for s in range(depth):
        parts[s][levels] = jnp.concatenate([high, low], axis=1)


def gather_kernel(depth, scale, place, *refs):
    slabs, mixed = refs[:depth], refs[depth]
    levels = mixed.shape[1]
    per = slabs[0].shape[2] // 128
    for s in range(depth):
        origin = lax.rem(place[0] + depth - s, depth)
        for i in range(per):
            mixed[origin * per + i] = slabs[s][:levels, :, i * 128 : (i + 1) * 128]
    if len(refs) > depth + 1:
        terms, message = refs[depth + 1 :]
        total = jnp.zeros(terms.shape, jnp.float32)
        for s in range(depth):
            behind = slabs[s][levels].astype(jnp.float32)
            total = total + (behind[:, :128] + behind[:, 128:])
        total = jnp.broadcast_to(jnp.sum(total, axis=1, keepdims=True), terms.shape) * scale
        terms[...] = total
        high = total.astype(jnp.bfloat16)
        blocks = mixed.shape[0]
        message[:blocks] = mixed[...]
        message[blocks, 0] = high
        message[blocks, 1] = (total - high.astype(jnp.float32)).astype(jnp.bfloat16)
        for l in range(2, levels):
            message[blocks, l] = jnp.zeros_like(high)


def add_entries(entries, start, steps, weights, near, total, ready=None):
    levels = near.shape[1]
    zero = jnp.zeros(near.shape[2:], jnp.bfloat16)
    tracers = zero.shape[0]

    def step(i, loaded):
        if ready is not None:
            last = entries[1, start + i * GROUP]
            for g in range(1, GROUP):
                last = jnp.maximum(last, entries[1, start + i * GROUP + g])
            loaded = ready(last + 1, loaded)
        found = []
        for g in range(GROUP):
            at = start + i * GROUP + g
            slot, block, source = entries[0, at], entries[1, at], entries[2, at]
            for l in range(0, levels, 2):
                lhs = jnp.concatenate(
                    [weights[block, l, slot], weights[block, l + 1, slot]], axis=1
                )
                rhs = jnp.concatenate(
                    [
                        jnp.concatenate([near[source, l], zero], axis=1),
                        jnp.concatenate([zero, near[source, l + 1]], axis=1),
                    ],
                    axis=0,
                )
                if g % 2:
                    lhs, rhs = rhs, lhs
                moved = lax.dot_general(
                    lhs, rhs, (((1,), (1,)), ((), ())), preferred_element_type=jnp.float32
                )
                found.append((g, block, l, moved))
        for g, block, l, moved in found:
            moved = moved if g % 2 else moved.T
            total[block, l] += moved[:tracers]
            total[block, l + 1] += moved[tracers:]
        return loaded

    return lax.fori_loop(0, steps, step, jnp.int32(AHEAD))


def near_kernel(load, place, entries, weights, own, mate, state, rates, coupling, *refs):
    if load:
        _, held, total, near, sem = refs
        state_in = state
    else:
        total, near, state_in, extra = refs
        held = weights
    blocks, levels, tracers, _ = own.shape
    odd = place[1]
    half = entries.shape[1] // 2
    if not load:
        copy = pltpu.make_async_copy(state, state_in, extra.at[0])
        copy.start()

    ready = None
    if load:

        def fetch(b):
            return pltpu.make_async_copy(weights.at[:, b], held.at[b], sem.at[b])

        def ready(needed, loaded):
            def finish(b, _):
                fetch(b).wait()
                return 0

            needed = jnp.maximum(needed, loaded)
            lax.fori_loop(loaded, needed, finish, 0)
            return needed

        for b in range(AHEAD, blocks):
            fetch(b).start()

    near[pl.ds(blocks, blocks)] = own[...]
    near[pl.ds((1 - odd) * 2 * blocks, blocks)] = mate[:blocks]
    near[3 * blocks] = jnp.zeros(near.shape[1:], near.dtype)

    def add_source():
        for b in range(blocks):
            lanes = slice(b * 128, (b + 1) * 128)
            values = jnp.concatenate([own[b, l] for l in range(levels)], axis=1)
            both = lax.dot_general(
                coupling[...], values, (((0,), (0,)), ((), ())), preferred_element_type=jnp.float32
            )
            both = both[:tracers] + both[tracers:]
            for l in range(levels):
                source = rates[l : l + 1, lanes] * both[:, l * 128 : (l + 1) * 128]
                total[b, l] += source - state_in[l, :, lanes].astype(jnp.float32)

    total[...] = jnp.zeros(total.shape, total.dtype)
    if load:
        add_source()
    steps = entries[0, 2 * half - 1]
    if not load:
        steps = lax.div(steps, 3)
    loaded = add_entries(entries, 0, steps, held, near, total, ready)
    if not load:
        copy.wait()
        add_source()
    if load:
        ready(blocks, loaded)


def rest_kernel(third, place, entries, weights, own, mate, before, total, near):
    blocks = own.shape[0]
    half = entries.shape[1] // 2
    near[pl.ds(blocks, blocks)] = own[...]
    near[pl.ds((1 - place[1]) * 2 * blocks, blocks)] = mate[:blocks]
    near[3 * blocks] = jnp.zeros(near.shape[1:], near.dtype)
    total[...] = before[...]
    steps = entries[0, 2 * half - 1]
    start, stop = lax.div(third * steps, 3), lax.div((third + 1) * steps, 3)
    add_entries(entries, start * GROUP, stop - start, weights, near, total)


def far_kernel(more, place, entries, weights, far, before, count, *refs):
    behind, out, parts = refs[:more], refs[more], refs[more + 1 : -4]
    near, total, new, sem = refs[-4:]
    blocks, levels, tracers, _ = far.shape
    half = entries.shape[1] // 2
    near[pl.ds(0, blocks)] = far[...]
    near[blocks] = jnp.zeros(near.shape[1:], near.dtype)
    total[...] = before[...]
    add_entries(entries, half, entries[1, 2 * half - 1], weights, near, total)
    copies = []
    for b in range(blocks):
        lanes = slice(b * 128, (b + 1) * 128)
        wet_levels = count[:, lanes] - place[0] * levels
        for l in range(levels):
            value = jnp.where(wet_levels > l, total[b, l], 0.0)
            new[l, :, lanes] = value.astype(jnp.bfloat16)
        here = pl.ds(b * 128, 128)
        copies.append(pltpu.make_async_copy(new.at[:, :, here], out.at[:, :, here], sem.at[b]))
        copies[-1].start()
    depth = len(parts)
    for s in range(depth):
        width = parts[s].shape[2]
        start = lax.rem(place[0] + s, depth) * width
        parts[s][:levels] = new[:, :, pl.ds(pl.multiple_of(start, width), width)]
    for passed_on in behind:
        parts[depth - 1][levels:] = passed_on[levels:]
    for copy in copies:
        copy.wait()


def ring(count, shift):
    return [(j, (j + shift) % count) for j in range(count)]


def exchange(parts, axis):
    count = len(parts)
    return [parts[0]] + [
        lax.ppermute(parts[s], axis, ring(count, s)) for s in range(1, count)
    ]


def params(mib):
    return pltpu.CompilerParams(vmem_limit_bytes=mib * MIB)


def cost(flops, size):
    return pl.CostEstimate(flops=flops, bytes_accessed=size, transcendentals=0)


def per_device(
    adjoint_seed, transport, neighbours, inv_mix, rates, coupling, sensitivity, depth_count
):
    tracers, levels, cols = adjoint_seed.shape
    blocks, slots = neighbours.shape
    horiz, depth = lax.axis_size("horiz"), lax.axis_size("depth")
    total_blocks = blocks * horiz
    h = lax.axis_index("horiz")
    place = jnp.stack([lax.axis_index("depth"), h % 2, h]).astype(jnp.int32)
    state = jnp.transpose(adjoint_seed, (1, 0, 2))
    sens = jnp.transpose(sensitivity, (1, 0, 2))
    count = depth_count.reshape(1, cols)
    scale = 1.0 / math.sqrt(levels * depth * total_blocks * 128)

    width = cols // depth
    block_shape = (blocks, levels, tracers, 128)
    terms_shape = jax.ShapeDtypeStruct((tracers, 128), jnp.float32)
    swap = [(i, i ^ 1) for i in range(horiz)]
    cross = []
    for i in range(1, horiz, 2):
        cross += [(i, (i + 1) % horiz), ((i + 1) % horiz, i)]

    def keep(value):
        return pltpu.with_memory_space_constraint(value, pltpu.VMEM)

    def leave(value):
        return pltpu.with_memory_space_constraint(value, pltpu.HBM)

    whole = jax.ShapeDtypeStruct((levels, tracers, cols), jnp.bfloat16)
    slab = jax.ShapeDtypeStruct((levels, tracers, width), jnp.bfloat16)
    longer = jax.ShapeDtypeStruct((levels + 1, tracers, width), jnp.bfloat16)
    total_shape = jax.ShapeDtypeStruct(block_shape, jnp.float32)
    partial_shape = jax.ShapeDtypeStruct((depth, levels, tracers, width), jnp.float32)
    mixed_scratch = pltpu.VMEM((depth, levels, tracers, width), jnp.bfloat16)

    def several(number):
        return jax.ShapeDtypeStruct((number * levels, tracers, width), jnp.bfloat16)

    *messages, own_state, own_sens, one_later, two_later, kept_state = pl.pallas_call(
        split_kernel,
        out_shape=[several(number) for number in (1, 1, 2, 1, 1, 1, 1)]
        + [pltpu.VMEM(whole.shape, jnp.bfloat16)],
        in_specs=[SMEM, HBM, HBM],
        out_specs=[VMEM] * 8,
        scratch_shapes=[
            pltpu.VMEM(whole.shape, jnp.bfloat16),
            pltpu.SemaphoreType.DMA((2,)),
        ],
        compiler_params=params(8),
        name="split",
    )(place, leave(state), leave(sens))
    slabs = exchange([own_state] + messages, "depth")
    inverse, rates, held = pl.pallas_call(
        prepare_kernel,
        out_shape=[
            pltpu.VMEM(inv_mix.shape, jnp.float32),
            pltpu.VMEM(rates.shape, jnp.float32),
            pltpu.VMEM((blocks, levels, slots, 128, 128), jnp.bfloat16),
        ],
        in_specs=[HBM] * 3,
        out_specs=[VMEM] * 3,
        scratch_shapes=[pltpu.SemaphoreType.DMA((2 + AHEAD,))],
        compiler_params=params(4),
        name="prepare",
    )(leave(inv_mix), leave(rates), leave(transport))

    def early(slab):
        return pl.pallas_call(
            early_kernel,
            out_shape=partial_shape,
            in_specs=[SMEM] + [VMEM] * 2,
            out_specs=VMEM,
            compiler_params=params(4),
            cost_estimate=cost(0, 3 * MIB),
            name="early",
        )(place, slab, keep(inverse))

    def gather(slabs, shapes):
        return pl.pallas_call(
            functools.partial(gather_kernel, depth, scale),
            out_shape=shapes,
            in_specs=[SMEM] + [VMEM] * depth,
            out_specs=[VMEM] * len(shapes),
            compiler_params=params(4),
            name="gather",
        )(place, *slabs)

    def move_far(far, total, shapes, *behind):
        return pl.pallas_call(
            functools.partial(far_kernel, len(behind)),
            out_shape=shapes,
            in_specs=[SMEM] * 2 + [VMEM] * (4 + len(behind)),
            out_specs=[HBM] + [VMEM] * (len(shapes) - 1),
            scratch_shapes=[
                pltpu.VMEM((blocks + 1,) + block_shape[1:], jnp.bfloat16),
                pltpu.VMEM(block_shape, jnp.float32),
                pltpu.VMEM(whole.shape, jnp.bfloat16),
                pltpu.SemaphoreType.DMA((blocks,)),
            ],
            compiler_params=params(4),
            cost_estimate=cost(0, 8 * MIB),
            name="far",
        )(place, entries, keep(held), keep(far), keep(total), keep(count), *behind)

    near_scratch = pltpu.VMEM((3 * blocks + 1,) + block_shape[1:], jnp.bfloat16)
    block_array = jax.ShapeDtypeStruct(block_shape, jnp.bfloat16)

    partial = early(slabs[0])
    three_sens = slabs[3]
    mixed = pl.pallas_call(
        functools.partial(mix_kernel, 2),
        out_shape=[several(number) for number in (1, 2, 1, 2)],
        in_specs=[SMEM] + [VMEM] * (depth + 3),
        out_specs=[VMEM] * depth,
        scratch_shapes=[mixed_scratch],
        compiler_params=params(4),
        name="mix",
    )(place, *slabs[1:], keep(inverse), keep(partial), one_later, two_later)
    slabs = exchange(mixed, "depth")
    one_sens = slabs[1]
    coupling, neighbours, _ = lax.optimization_barrier((coupling, neighbours, mixed))
    entries, pair, count = pl.pallas_call(
        functools.partial(list_kernel, total_blocks),
        out_shape=[
            jax.ShapeDtypeStruct((3, 128), jnp.int32),
            jax.ShapeDtypeStruct((tracers, 2 * tracers), jnp.bfloat16),
            jax.ShapeDtypeStruct(count.shape, count.dtype),
        ],
        in_specs=[SMEM, SMEM, VMEM, VMEM],
        out_specs=[SMEM, VMEM, VMEM],
        compiler_params=params(4),
        name="list",
    )(place, neighbours, coupling, count)
    slabs, entries, pair = lax.optimization_barrier((slabs, entries, pair))
    (own,) = gather(slabs, [block_array])
    mate = lax.ppermute(own, "horiz", swap)
    far = lax.ppermute(own, "horiz", cross)
    held, total = pl.pallas_call(
        functools.partial(near_kernel, True),
        out_shape=[
            pltpu.VMEM((blocks, levels, slots, 128, 128), jnp.bfloat16),
            total_shape,
        ],
        in_specs=[SMEM, SMEM, HBM] + [VMEM] * 6,
        out_specs=[VMEM, VMEM],
        input_output_aliases={8: 0},
        scratch_shapes=[near_scratch, pltpu.SemaphoreType.DMA((blocks,))],
        compiler_params=params(4),
        cost_estimate=cost(0, 16 * MIB),
        name="near_load",
    )(
        place, entries, leave(transport), keep(own), keep(mate),
        keep(kept_state), keep(rates), pair, keep(held),
    )
    shapes = [whole] + [slab] * (depth - 1) + [several(2)]
    first, *parts = move_far(far, total, shapes, slabs[3])

    slabs = exchange(parts, "depth")
    partial = early(slabs[0])
    terms = pl.pallas_call(
        weigh_kernel,
        out_shape=terms_shape,
        in_specs=[SMEM] + [VMEM] * 7,
        out_specs=VMEM,
        compiler_params=params(4),
        name="weigh",
    )(place, mixed[0], mixed[1], mixed[3], own_sens, one_sens, three_sens, count)
    parts = pl.pallas_call(
        mix_last_kernel,
        out_shape=[longer] * depth,
        in_specs=[SMEM] + [VMEM] * (depth + 7),
        out_specs=[VMEM] * depth,
        scratch_shapes=[mixed_scratch],
        compiler_params=params(4),
        name="mix_last",
    )(
        place, *slabs[1:], keep(inverse), keep(partial),
        own_sens, one_sens, three_sens, mixed[2], keep(count), terms,
    )
    slabs = exchange(parts, "depth")
    message_shape = jax.ShapeDtypeStruct((blocks + 1,) + block_shape[1:], jnp.bfloat16)
    own, terms, message = gather(slabs, [block_array, terms_shape, message_shape])
    mate = lax.ppermute(message, "horiz", swap)
    far = lax.ppermute(own, "horiz", cross)

    def add_pairs(terms, flip):
        return terms + lax.ppermute(terms, "horiz", [(i, i ^ flip) for i in range(horiz)])

    terms = terms + (mate[blocks, 0].astype(jnp.float32) + mate[blocks, 1].astype(jnp.float32))
    terms, own, mate = lax.optimization_barrier((terms, own, mate))
    total = pl.pallas_call(
        functools.partial(near_kernel, False),
        out_shape=total_shape,
        in_specs=[SMEM, SMEM, VMEM, VMEM, VMEM, HBM, VMEM, VMEM],
        out_specs=VMEM,
        scratch_shapes=[
            near_scratch,
            pltpu.VMEM(whole.shape, jnp.bfloat16),
            pltpu.SemaphoreType.DMA((1,)),
        ],
        compiler_params=params(4),
        cost_estimate=cost(0, 10 * MIB),
        name="near",
    )(place, entries, keep(held), keep(own), keep(mate), leave(first), keep(rates), pair)
    terms = add_pairs(terms, 7)
    terms, total = lax.optimization_barrier((terms, total))
    for third, flip in ((1, 25), (2, 9)):
        total = pl.pallas_call(
            functools.partial(rest_kernel, third),
            out_shape=total_shape,
            in_specs=[SMEM, SMEM] + [VMEM] * 4,
            out_specs=VMEM,
            scratch_shapes=[near_scratch],
            compiler_params=params(4),
            cost_estimate=cost(0, 10 * MIB),
            name="rest",
        )(place, entries, keep(held), keep(own), keep(mate), keep(total))
        terms = add_pairs(terms, flip)
        terms, total = lax.optimization_barrier((terms, total))
    (second,) = move_far(far, total, [whole])
    terms = add_pairs(terms, 3)
    gradient = terms[:, 0]
    return (jnp.transpose(first, (1, 0, 2)), jnp.transpose(second, (1, 0, 2)), gradient)


def solution(mesh):
    return jax.shard_map(
        per_device,
        mesh=mesh,
        in_specs=(
            P(None, "depth", "horiz"),
            P("depth", "horiz", None, None, None),
            P("horiz", None),
            P(None, None, ("horiz", "depth")),
            P("depth", "horiz"),
            P(),
            P(None, "depth", "horiz"),
            P("horiz"),
        ),
        out_specs=(P(None, "depth", "horiz"), P(None, "depth", "horiz"), P()),
        check_vma=False,
    )
```

```python
import functools
import math

import jax
import jax.numpy as jnp
from jax import lax
from jax.experimental import pallas as pl
from jax.experimental.pallas import tpu as pltpu
from jax.sharding import PartitionSpec as P

VMEM = pl.BlockSpec(memory_space=pltpu.VMEM)
SMEM = pl.BlockSpec(memory_space=pltpu.SMEM)
HBM = pl.BlockSpec(memory_space=pltpu.HBM)
MIB = 1024 * 1024
AHEAD = 3
GROUP = 4


def split_kernel(place, state, sens, *refs):
    one, two, three, own, own_sens, later_one, later_two, kept, held, sem = refs
    levels, _, width = own.shape
    depth = state.shape[2] // width
    copies = [
        pltpu.make_async_copy(state, kept, sem.at[0]),
        pltpu.make_async_copy(sens, held, sem.at[1]),
    ]
    for copy in copies:
        copy.start()
    for i, targets in enumerate(
        (
            ((own, 0, 0), (one, 0, 1), (two, 0, 2), (three, 0, 3)),
            ((own_sens, 0, 0), (later_one, 0, 1), (later_two, 0, 2), (three, 1, 3)),
        )
    ):
        copies[i].wait()
        for part, at, s in targets:
            start = lax.rem(place[0] + s, depth) * width
            whole = (kept, held)[i]
            part[at * levels : (at + 1) * levels] = whole[
                :, :, pl.ds(pl.multiple_of(start, width), width)
            ]


def list_entries(place, neighbours, entries, total_blocks):
    blocks, slots = neighbours.shape
    half = entries.shape[1] // 2
    odd = place[1]
    shift = 2 * blocks * odd
    counts = (jnp.int32(0), jnp.int32(0))
    for b in range(blocks):
        row = place[2] * blocks + (b - blocks)
        for k in range(slots):
            ahead = neighbours[b, k] - row
            ahead = jnp.where(ahead < 0, ahead + total_blocks, ahead)
            ahead = jnp.where(ahead >= total_blocks, ahead - total_blocks, ahead)
            source = b + jnp.clip(ahead, 0, 2 * blocks)
            inside = source - shift
            far = jnp.where((inside >= 0) & (inside < blocks), 1, 0)
            at = jnp.where(far == 1, half + counts[1], counts[0])
            entries[0, at] = k
            entries[1, at] = b
            entries[2, at] = jnp.where(far == 1, inside, source)
            counts = (counts[0] + 1 - far, counts[1] + far)
    for begin, number, none in ((0, counts[0], 3 * blocks), (half, counts[1], blocks)):
        for g in range(GROUP - 1):
            entries[0, begin + number + g] = 0
            entries[1, begin + number + g] = 0
            entries[2, begin + number + g] = none
    entries[0, 2 * half - 1] = lax.div(counts[0] + GROUP - 1, GROUP)
    entries[1, 2 * half - 1] = lax.div(counts[1] + GROUP - 1, GROUP)
    entries[2, half - 1] = counts[0]
    entries[2, 2 * half - 1] = counts[1]


def prepare_kernel(inverse, rates, weights, held, held_rates, held_weights, sem):
    copies = [
        pltpu.make_async_copy(inverse, held, sem.at[0]),
        pltpu.make_async_copy(rates, held_rates, sem.at[1]),
    ]
    for b in range(AHEAD):
        copies.append(pltpu.make_async_copy(weights.at[:, b], held_weights.at[b], sem.at[2 + b]))
    for copy in copies:
        copy.start()
    for copy in copies:
        copy.wait()


def list_kernel(total_blocks, place, neighbours, coupling, count, entries, pair, count_out):
    high = coupling[...].astype(jnp.bfloat16)
    low = (coupling[...] - high.astype(jnp.float32)).astype(jnp.bfloat16)
    pair[...] = jnp.concatenate([high, low], axis=1)
    count_out[...] = count[...]
    list_entries(place, neighbours, entries, total_blocks)


def add_products(place, slabs, steps, inverse, totals, target, lanes, levels):
    depth = inverse.shape[0] // levels
    for slab, s in zip(slabs, steps):
        base = lax.rem(place[0] + depth - s, depth) * levels

        def add(p, totals):
            value = slab[p, :, lanes].astype(jnp.float32)
            rows = inverse[base + p, target * levels : (target + 1) * levels, lanes]
            return tuple(t + rows[q : q + 1] * value for q, t in enumerate(totals))

        totals = lax.fori_loop(0, levels, add, totals, unroll=levels)
    return totals


def early_kernel(place, slab, inverse, partial):
    levels, tracers, cols = slab.shape
    for target in range(inverse.shape[0] // levels):
        for lane in range(0, cols, 128):
            lanes = slice(lane, lane + 128)
            totals = tuple(jnp.zeros((tracers, 128), jnp.float32) for _ in range(levels))
            totals = add_products(place, [slab], [0], inverse, totals, target, lanes, levels)
            for q in range(levels):
                partial[target, q, :, lanes] = totals[q]


def weigh(place, pairs, count):
    total = None
    for s, mixed, sens in pairs:
        levels, _, cols = pairs[0][2].shape
        depth = count.shape[1] // cols
        offset = sens.shape[0] - levels
        target = lax.rem(place[0] + depth - s, depth)
        for lane in range(0, cols, 128):
            lanes = slice(lane, lane + 128)
            here = pl.ds(pl.multiple_of(place[0] * cols + lane, 128), 128)
            wet_levels = count[:, here] - target * levels
            for q in range(levels):
                value = sum(part[q, :, lanes].astype(jnp.float32) for part in mixed)
                product = value * sens[offset + q, :, lanes].astype(jnp.float32)
                product = jnp.where(wet_levels > q, product, 0.0)
                total = product if total is None else total + product
    return total


def weigh_kernel(place, *refs):
    own, one, three, own_sens, one_sens, three_sens, count, terms = refs
    pairs = ((0, [own], own_sens), (1, [three], one_sens), (3, [one], three_sens))
    terms[...] = weigh(place, pairs, count)


def mix_kernel(number, place, *refs):
    mixed = refs[-1]
    depth, levels, tracers, cols = mixed.shape
    slabs, inverse, partial = refs[: depth - 1], refs[depth - 1], refs[depth]
    parts = refs[-1 - depth : -1]
    for target in range(depth):
        at = lax.rem(target - place[0] + depth, depth)
        for lane in range(0, cols, 128):
            lanes = slice(lane, lane + 128)
            totals = tuple(partial[target, q, :, lanes] for q in range(levels))
            totals = add_products(
                place, slabs, range(1, depth), inverse, totals, target, lanes, levels
            )
            for q in range(levels):
                mixed[at, q, :, lanes] = totals[q].astype(jnp.bfloat16)
    for s in range(depth):
        parts[s][:levels] = mixed[s]
    for i in range(number):
        parts[2 * i + 1][levels:] = refs[depth + 1 + i][...]


def mix_last_kernel(place, *refs):
    mixed = refs[-1]
    depth, levels = mixed.shape[:2]
    own_sens, one_sens, three_sens, early_mixed, count, before = refs[depth + 1 : depth + 7]
    parts = refs[-1 - depth : -1]
    mix_kernel(0, place, *refs[: depth + 1], *parts, mixed)
    pairs = (
        (0, [mixed.at[0]], own_sens),
        (1, [mixed.at[3]], one_sens),
        (2, [mixed.at[2], early_mixed], refs[2]),
        (3, [mixed.at[1]], three_sens),
    )
    terms = before[...] + weigh(place, pairs, count)
    high = terms.astype(jnp.bfloat16)
    low = (terms - high.astype(jnp.float32)).astype(jnp.bfloat16)
    for s in range(depth):
        parts[s][levels] = jnp.concatenate([high, low], axis=1)
        for l in range(levels + 1, parts[s].shape[0]):
            parts[s][l] = jnp.zeros(parts[s].shape[1:], parts[s].dtype)


def gather_kernel(depth, scale, place, *refs):
    slabs, mixed = refs[:depth], refs[depth]
    levels = mixed.shape[1]
    per = slabs[0].shape[2] // 128
    for s in range(depth):
        origin = lax.rem(place[0] + depth - s, depth)
        for i in range(per):
            mixed[origin * per + i] = slabs[s][:levels, :, i * 128 : (i + 1) * 128]
    if len(refs) > depth + 1:
        terms, message = refs[depth + 1 :]
        total = jnp.zeros(terms.shape, jnp.float32)
        for s in range(depth):
            behind = slabs[s][levels].astype(jnp.float32)
            total = total + (behind[:, :128] + behind[:, 128:])
        total = jnp.broadcast_to(jnp.sum(total, axis=1, keepdims=True), terms.shape) * scale
        terms[...] = total
        high = total.astype(jnp.bfloat16)
        blocks = mixed.shape[0]
        message[:blocks] = mixed[...]
        message[blocks, 0] = high
        message[blocks, 1] = (total - high.astype(jnp.float32)).astype(jnp.bfloat16)
        for l in range(2, levels):
            message[blocks, l] = jnp.zeros_like(high)


def add_entries(entries, start, steps, weights, near, total, ready=None):
    levels = near.shape[1]
    zero = jnp.zeros(near.shape[2:], jnp.bfloat16)
    tracers = zero.shape[0]

    def step(i, loaded):
        if ready is not None:
            last = entries[1, start + i * GROUP]
            for g in range(1, GROUP):
                last = jnp.maximum(last, entries[1, start + i * GROUP + g])
            loaded = ready(last + 1, loaded)
        found = []
        for g in range(GROUP):
            at = start + i * GROUP + g
            slot, block, source = entries[0, at], entries[1, at], entries[2, at]
            for l in range(0, levels, 2):
                lhs = jnp.concatenate(
                    [weights[block, l, slot], weights[block, l + 1, slot]], axis=1
                )
                rhs = jnp.concatenate(
                    [
                        jnp.concatenate([near[source, l], zero], axis=1),
                        jnp.concatenate([zero, near[source, l + 1]], axis=1),
                    ],
                    axis=0,
                )
                if g % 2:
                    lhs, rhs = rhs, lhs
                moved = lax.dot_general(
                    lhs, rhs, (((1,), (1,)), ((), ())), preferred_element_type=jnp.float32
                )
                found.append((g, block, l, moved))
        for g, block, l, moved in found:
            moved = moved if g % 2 else moved.T
            total[block, l] += moved[:tracers]
            total[block, l + 1] += moved[tracers:]
        return loaded

    return lax.fori_loop(0, steps, step, jnp.int32(AHEAD))


def near_kernel(load, place, entries, weights, own, mate, state, rates, coupling, *refs):
    if load:
        _, held, total, near, sem = refs
        state_in = state
    else:
        total, near, state_in, extra = refs
        held = weights
    blocks, levels, tracers, _ = own.shape
    odd = place[1]
    half = entries.shape[1] // 2
    if not load:
        copy = pltpu.make_async_copy(state, state_in, extra.at[0])
        copy.start()

    ready = None
    if load:

        def fetch(b):
            return pltpu.make_async_copy(weights.at[:, b], held.at[b], sem.at[b])

        def ready(needed, loaded):
            def finish(b, _):
                fetch(b).wait()
                return 0

            needed = jnp.maximum(needed, loaded)
            lax.fori_loop(loaded, needed, finish, 0)
            return needed

        for b in range(AHEAD, blocks):
            fetch(b).start()

    near[pl.ds(blocks, blocks)] = own[...]
    near[pl.ds((1 - odd) * 2 * blocks, blocks)] = mate[:blocks]
    near[3 * blocks] = jnp.zeros(near.shape[1:], near.dtype)

    def add_source():
        for b in range(blocks):
            lanes = slice(b * 128, (b + 1) * 128)
            values = jnp.concatenate([own[b, l] for l in range(levels)], axis=1)
            both = lax.dot_general(
                coupling[...], values, (((0,), (0,)), ((), ())), preferred_element_type=jnp.float32
            )
            both = both[:tracers] + both[tracers:]
            for l in range(levels):
                source = rates[l : l + 1, lanes] * both[:, l * 128 : (l + 1) * 128]
                total[b, l] += source - state_in[l, :, lanes].astype(jnp.float32)

    total[...] = jnp.zeros(total.shape, total.dtype)
    if load:
        add_source()
    steps = entries[0, 2 * half - 1]
    if not load:
        steps = lax.div(steps, 3)
    loaded = add_entries(entries, 0, steps, held, near, total, ready)
    if not load:
        copy.wait()
        add_source()
    if load:
        ready(blocks, loaded)


def rest_kernel(third, place, entries, weights, own, mate, before, total, near):
    blocks = own.shape[0]
    half = entries.shape[1] // 2
    near[pl.ds(blocks, blocks)] = own[...]
    near[pl.ds((1 - place[1]) * 2 * blocks, blocks)] = mate[:blocks]
    near[3 * blocks] = jnp.zeros(near.shape[1:], near.dtype)
    total[...] = before[...]
    steps = entries[0, 2 * half - 1]
    start, stop = lax.div(third * steps, 3), lax.div((third + 1) * steps, 3)
    add_entries(entries, start * GROUP, stop - start, weights, near, total)


def far_kernel(more, place, entries, weights, far, before, count, *refs):
    behind, out, parts = refs[:more], refs[more], refs[more + 1 : -4]
    near, total, new, sem = refs[-4:]
    blocks, levels, tracers, _ = far.shape
    half = entries.shape[1] // 2
    near[pl.ds(0, blocks)] = far[...]
    near[blocks] = jnp.zeros(near.shape[1:], near.dtype)
    total[...] = before[...]
    add_entries(entries, half, entries[1, 2 * half - 1], weights, near, total)
    copies = []
    for b in range(blocks):
        lanes = slice(b * 128, (b + 1) * 128)
        wet_levels = count[:, lanes] - place[0] * levels
        for l in range(levels):
            value = jnp.where(wet_levels > l, total[b, l], 0.0)
            new[l, :, lanes] = value.astype(jnp.bfloat16)
        here = pl.ds(b * 128, 128)
        copies.append(pltpu.make_async_copy(new.at[:, :, here], out.at[:, :, here], sem.at[b]))
        copies[-1].start()
    depth = len(parts)
    for s in range(depth):
        width = parts[s].shape[2]
        start = lax.rem(place[0] + s, depth) * width
        parts[s][:levels] = new[:, :, pl.ds(pl.multiple_of(start, width), width)]
    for passed_on in behind:
        parts[depth - 1][levels:] = passed_on[levels:]
    for copy in copies:
        copy.wait()


def ring(count, shift):
    return [(j, (j + shift) % count) for j in range(count)]


def exchange(parts, axis):
    count = len(parts)
    return [parts[0]] + [
        lax.ppermute(parts[s], axis, ring(count, s)) for s in range(1, count)
    ]


def params(mib):
    return pltpu.CompilerParams(vmem_limit_bytes=mib * MIB)


def cost(flops, size):
    return pl.CostEstimate(flops=flops, bytes_accessed=size, transcendentals=0)


def per_device(
    adjoint_seed, transport, neighbours, inv_mix, rates, coupling, sensitivity, depth_count
):
    tracers, levels, cols = adjoint_seed.shape
    blocks, slots = neighbours.shape
    horiz, depth = lax.axis_size("horiz"), lax.axis_size("depth")
    total_blocks = blocks * horiz
    h = lax.axis_index("horiz")
    place = jnp.stack([lax.axis_index("depth"), h % 2, h]).astype(jnp.int32)
    state = jnp.transpose(adjoint_seed, (1, 0, 2))
    sens = jnp.transpose(sensitivity, (1, 0, 2))
    count = depth_count.reshape(1, cols)
    scale = 1.0 / math.sqrt(levels * depth * total_blocks * 128)

    width = cols // depth
    block_shape = (blocks, levels, tracers, 128)
    terms_shape = jax.ShapeDtypeStruct((tracers, 128), jnp.float32)
    swap = [(i, i ^ 1) for i in range(horiz)]
    cross = []
    for i in range(1, horiz, 2):
        cross += [(i, (i + 1) % horiz), ((i + 1) % horiz, i)]

    def keep(value):
        return pltpu.with_memory_space_constraint(value, pltpu.VMEM)

    def leave(value):
        return pltpu.with_memory_space_constraint(value, pltpu.HBM)

    whole = jax.ShapeDtypeStruct((levels, tracers, cols), jnp.bfloat16)
    slab = jax.ShapeDtypeStruct((levels, tracers, width), jnp.bfloat16)
    longest = jax.ShapeDtypeStruct((levels + 2, tracers, width), jnp.bfloat16)
    longer = jax.ShapeDtypeStruct((levels + 1, tracers, width), jnp.bfloat16)
    total_shape = jax.ShapeDtypeStruct(block_shape, jnp.float32)
    partial_shape = jax.ShapeDtypeStruct((depth, levels, tracers, width), jnp.float32)
    mixed_scratch = pltpu.VMEM((depth, levels, tracers, width), jnp.bfloat16)

    def several(number):
        return jax.ShapeDtypeStruct((number * levels, tracers, width), jnp.bfloat16)

    *messages, own_state, own_sens, one_later, two_later, kept_state = pl.pallas_call(
        split_kernel,
        out_shape=[several(number) for number in (1, 1, 2, 1, 1, 1, 1)]
        + [pltpu.VMEM(whole.shape, jnp.bfloat16)],
        in_specs=[SMEM, HBM, HBM],
        out_specs=[VMEM] * 8,
        scratch_shapes=[
            pltpu.VMEM(whole.shape, jnp.bfloat16),
            pltpu.SemaphoreType.DMA((2,)),
        ],
        compiler_params=params(8),
        name="split",
    )(place, leave(state), leave(sens))
    slabs = exchange([own_state] + messages, "depth")
    inverse, rates, held = pl.pallas_call(
        prepare_kernel,
        out_shape=[
            pltpu.VMEM(inv_mix.shape, jnp.float32),
            pltpu.VMEM(rates.shape, jnp.float32),
            pltpu.VMEM((blocks, levels, slots, 128, 128), jnp.bfloat16),
        ],
        in_specs=[HBM] * 3,
        out_specs=[VMEM] * 3,
        scratch_shapes=[pltpu.SemaphoreType.DMA((2 + AHEAD,))],
        compiler_params=params(4),
        name="prepare",
    )(leave(inv_mix), leave(rates), leave(transport))

    def early(slab):
        return pl.pallas_call(
            early_kernel,
            out_shape=partial_shape,
            in_specs=[SMEM] + [VMEM] * 2,
            out_specs=VMEM,
            compiler_params=params(4),
            cost_estimate=cost(0, 3 * MIB),
            name="early",
        )(place, slab, keep(inverse))

    def gather(slabs, shapes):
        return pl.pallas_call(
            functools.partial(gather_kernel, depth, scale),
            out_shape=shapes,
            in_specs=[SMEM] + [VMEM] * depth,
            out_specs=[VMEM] * len(shapes),
            compiler_params=params(4),
            name="gather",
        )(place, *slabs)

    def move_far(far, total, shapes, *behind):
        return pl.pallas_call(
            functools.partial(far_kernel, len(behind)),
            out_shape=shapes,
            in_specs=[SMEM] * 2 + [VMEM] * (4 + len(behind)),
            out_specs=[HBM] + [VMEM] * (len(shapes) - 1),
            scratch_shapes=[
                pltpu.VMEM((blocks + 1,) + block_shape[1:], jnp.bfloat16),
                pltpu.VMEM(block_shape, jnp.float32),
                pltpu.VMEM(whole.shape, jnp.bfloat16),
                pltpu.SemaphoreType.DMA((blocks,)),
            ],
            compiler_params=params(4),
            cost_estimate=cost(0, 8 * MIB),
            name="far",
        )(place, entries, keep(held), keep(far), keep(total), keep(count), *behind)

    near_scratch = pltpu.VMEM((3 * blocks + 1,) + block_shape[1:], jnp.bfloat16)
    block_array = jax.ShapeDtypeStruct(block_shape, jnp.bfloat16)

    partial = early(slabs[0])
    three_sens = slabs[3]
    mixed = pl.pallas_call(
        functools.partial(mix_kernel, 2),
        out_shape=[several(number) for number in (1, 2, 1, 2)],
        in_specs=[SMEM] + [VMEM] * (depth + 3),
        out_specs=[VMEM] * depth,
        scratch_shapes=[mixed_scratch],
        compiler_params=params(4),
        name="mix",
    )(place, *slabs[1:], keep(inverse), keep(partial), one_later, two_later)
    slabs = exchange(mixed, "depth")
    one_sens = slabs[1]
    coupling, neighbours, _ = lax.optimization_barrier((coupling, neighbours, mixed))
    entries, pair, count = pl.pallas_call(
        functools.partial(list_kernel, total_blocks),
        out_shape=[
            jax.ShapeDtypeStruct((3, 128), jnp.int32),
            jax.ShapeDtypeStruct((tracers, 2 * tracers), jnp.bfloat16),
            jax.ShapeDtypeStruct(count.shape, count.dtype),
        ],
        in_specs=[SMEM, SMEM, VMEM, VMEM],
        out_specs=[SMEM, VMEM, VMEM],
        compiler_params=params(4),
        name="list",
    )(place, neighbours, coupling, count)
    slabs, entries, pair = lax.optimization_barrier((slabs, entries, pair))
    (own,) = gather(slabs, [block_array])
    mate = lax.ppermute(own, "horiz", swap)
    far = lax.ppermute(own, "horiz", cross)
    held, total = pl.pallas_call(
        functools.partial(near_kernel, True),
        out_shape=[
            pltpu.VMEM((blocks, levels, slots, 128, 128), jnp.bfloat16),
            total_shape,
        ],
        in_specs=[SMEM, SMEM, HBM] + [VMEM] * 6,
        out_specs=[VMEM, VMEM],
        input_output_aliases={8: 0},
        scratch_shapes=[near_scratch, pltpu.SemaphoreType.DMA((blocks,))],
        compiler_params=params(4),
        cost_estimate=cost(0, 16 * MIB),
        name="near_load",
    )(
        place, entries, leave(transport), keep(own), keep(mate),
        keep(kept_state), keep(rates), pair, keep(held),
    )
    shapes = [whole] + [slab] * (depth - 1) + [several(2)]
    first, *parts = move_far(far, total, shapes, slabs[3])

    slabs = exchange(parts, "depth")
    partial = early(slabs[0])
    terms = pl.pallas_call(
        weigh_kernel,
        out_shape=terms_shape,
        in_specs=[SMEM] + [VMEM] * 7,
        out_specs=VMEM,
        compiler_params=params(4),
        name="weigh",
    )(place, mixed[0], mixed[1], mixed[3], own_sens, one_sens, three_sens, count)
    parts = pl.pallas_call(
        mix_last_kernel,
        out_shape=[longer, longer, longest, longer],
        in_specs=[SMEM] + [VMEM] * (depth + 7),
        out_specs=[VMEM] * depth,
        scratch_shapes=[mixed_scratch],
        compiler_params=params(4),
        name="mix_last",
    )(
        place, *slabs[1:], keep(inverse), keep(partial),
        own_sens, one_sens, three_sens, mixed[2], keep(count), terms,
    )
    slabs = exchange(parts, "depth")
    message_shape = jax.ShapeDtypeStruct((blocks + 1,) + block_shape[1:], jnp.bfloat16)
    own, terms, message = gather(slabs, [block_array, terms_shape, message_shape])
    mate = lax.ppermute(message, "horiz", swap)
    far = lax.ppermute(own, "horiz", cross)

    def add_pairs(terms, flip):
        return terms + lax.ppermute(terms, "horiz", [(i, i ^ flip) for i in range(horiz)])

    terms = terms + (mate[blocks, 0].astype(jnp.float32) + mate[blocks, 1].astype(jnp.float32))
    terms, own, mate = lax.optimization_barrier((terms, own, mate))
    total = pl.pallas_call(
        functools.partial(near_kernel, False),
        out_shape=total_shape,
        in_specs=[SMEM, SMEM, VMEM, VMEM, VMEM, HBM, VMEM, VMEM],
        out_specs=VMEM,
        scratch_shapes=[
            near_scratch,
            pltpu.VMEM(whole.shape, jnp.bfloat16),
            pltpu.SemaphoreType.DMA((1,)),
        ],
        compiler_params=params(4),
        cost_estimate=cost(0, 10 * MIB),
        name="near",
    )(place, entries, keep(held), keep(own), keep(mate), leave(first), keep(rates), pair)
    terms = add_pairs(terms, 7)
    terms, total = lax.optimization_barrier((terms, total))
    for third, flip in ((1, 25), (2, 9)):
        total = pl.pallas_call(
            functools.partial(rest_kernel, third),
            out_shape=total_shape,
            in_specs=[SMEM, SMEM] + [VMEM] * 4,
            out_specs=VMEM,
            scratch_shapes=[near_scratch],
            compiler_params=params(4),
            cost_estimate=cost(0, 10 * MIB),
            name="rest",
        )(place, entries, keep(held), keep(own), keep(mate), keep(total))
        terms = add_pairs(terms, flip)
        terms, total = lax.optimization_barrier((terms, total))
    (second,) = move_far(far, total, [whole])
    terms = add_pairs(terms, 3)
    gradient = terms[:, 0]
    return (jnp.transpose(first, (1, 0, 2)), jnp.transpose(second, (1, 0, 2)), gradient)


def solution(mesh):
    return jax.shard_map(
        per_device,
        mesh=mesh,
        in_specs=(
            P(None, "depth", "horiz"),
            P("depth", "horiz", None, None, None),
            P("horiz", None),
            P(None, None, ("horiz", "depth")),
            P("depth", "horiz"),
            P(),
            P(None, "depth", "horiz"),
            P("horiz"),
        ),
        out_specs=(P(None, "depth", "horiz"), P(None, "depth", "horiz"), P()),
        check_vma=False,
    )
```
